32 devices in a mesh: row: 4 (over z), col: 8 (over y, x, core).
Axes of the slice: x: 2, y: 2, z: 4, core: 2. Of those that a mesh axis runs over, the one named last changes fastest.
Arguments:
- matrix_tiles: bfloat16 [4, 8, 384, 128, 128], P('row', 'col')
- row_coords: int32 [4, 8, 384], P('row', 'col'), may hold values from 0 to 2047, as said below
- col_coords: int32 [4, 8, 384], P('row', 'col'), may hold values from 0 to 1023, as said below
- left_basis: float32 [8, 8192, 128], P(None, ('row', 'col'))
- right_basis: float32 [8, 8192, 128], P(None, ('col', 'row'))
Outputs:
- new_left: float32 [2, 8192, 128], P(None, ('row', 'col'))
- new_right: float32 [2, 8192, 128], P(None, ('col', 'row'))
- bidiagonal: float32 [2, 2], replicated
The draws below stay inside these ranges and needn't reach their ends.
Inputs may be any that keep to these rules, and one draw needn't show every extreme that they name: `row_coords`: slot s of a device lies in row blocks 256 * a to 256 * a + 255 of its row group, with a = s // 48. `col_coords`: slot s of a device lies in column blocks 256 * b to 256 * b + 255 of its column group, with b = (s // 12) % 4.
All inputs are finite; a program needn't handle non-finite values.
Results may differ from the reference program's by a relative error of at most 0.0012.
Values may be sent and summed in bfloat16 or wider, within the bound.
A program may use at most 64 MiB of HBM per device.

```python
import math
import jax
import jax.numpy as jnp
from jax import lax

BS = 128
KB = 8
ITERS = 2
SLOTS = 384
BLK_DEV = 256
RGB = 2048
CGB = 1024
MB = 8192
N_ROW = 4
N_COL = 8


def draw_matrix_tiles(key, part):
    key_noise = jax.random.fold_in(key, 11)
    key_scale = jax.random.fold_in(key, 12)
    dims_all = (N_ROW, N_COL, SLOTS, BS, BS)
    random_part = jax.random.normal(key_noise, dims_all, jnp.float32)
    offset = 0.5
    tile_scale = jnp.exp(jax.random.uniform(key_scale, (N_ROW, N_COL, SLOTS, 1, 1), jnp.float32, 0.0, math.log(10.0)))
    position = (jnp.arange(N_ROW)[:, None] * N_COL + jnp.arange(N_COL)[None, :]).astype(jnp.float32)
    position = position / max(N_ROW * N_COL - 1, 1)
    rising = jnp.power(3.0, position)[:, :, None, None, None]
    return (0.012 * tile_scale * rising * (random_part + offset)).astype(jnp.bfloat16)


def draw_row_coords(key, part):
    key_rows = jax.random.fold_in(key, 31)
    owners = jnp.arange(SLOTS, dtype=jnp.int32) // (SLOTS // N_COL)
    offsets = jax.random.randint(key_rows, (N_ROW, N_COL, SLOTS), 0, BLK_DEV, dtype=jnp.int32)
    return (owners[None, None, :] * BLK_DEV + offsets).astype(jnp.int32)


def draw_col_coords(key, part):
    key_cols = jax.random.fold_in(key, 32)
    owners = jnp.arange(SLOTS, dtype=jnp.int32) // (SLOTS // (N_ROW * N_COL)) % N_ROW
    offsets = jax.random.randint(key_cols, (N_ROW, N_COL, SLOTS), 0, BLK_DEV, dtype=jnp.int32)
    return (owners[None, None, :] * BLK_DEV + offsets).astype(jnp.int32)


def walsh_basis(key, salt):
    key_noise = jax.random.fold_in(key, salt)
    random_part = jax.random.normal(key_noise, (KB, MB, BS), jnp.float32)
    weight = 0.6
    region = jnp.arange(MB, dtype=jnp.int32) * KB // MB
    order = KB - 1 - jnp.arange(KB, dtype=jnp.int32)
    shared = jnp.bitwise_and(order[:, None], region[None, :])
    parity = jnp.zeros((KB, MB), jnp.int32)
    for bit_pos in range(KB.bit_length() - 1):
        parity = parity + jnp.bitwise_and(jnp.right_shift(shared, bit_pos), 1)
    pattern = (1 - 2 * jnp.bitwise_and(parity, 1)).astype(jnp.float32)
    return (weight * pattern[:, :, None] + math.sqrt(1.0 - weight * weight) * random_part).astype(jnp.float32)


def draw_left_basis(key, part):
    return walsh_basis(key, 21)


def draw_right_basis(key, part):
    return walsh_basis(key, 22)


def setup_inputs(seed: int = 0) -> dict:
    key_list = jax.random.split(jax.random.key(seed), 6)
    matrix_tiles = draw_matrix_tiles(jax.random.fold_in(key_list[5], 71), 0)
    row_coords = draw_row_coords(jax.random.fold_in(key_list[5], 71), 0)
    col_coords = draw_col_coords(jax.random.fold_in(key_list[5], 71), 0)
    left_basis = draw_left_basis(jax.random.fold_in(key_list[5], 71), 0)
    right_basis = draw_right_basis(jax.random.fold_in(key_list[5], 71), 0)
    return dict(matrix_tiles=matrix_tiles, row_coords=row_coords, col_coords=col_coords, left_basis=left_basis, right_basis=right_basis)


eps_floor = 1e-06
highest = lax.Precision.HIGHEST

def apply_matrix(matrix_tiles, row_coords, col_coords, vector, transposed):
    flat_tiles = matrix_tiles.reshape(N_ROW * N_COL, SLOTS, BS, BS)
    flat_rows = row_coords.reshape(N_ROW * N_COL, SLOTS)
    flat_cols = col_coords.reshape(N_ROW * N_COL, SLOTS)
    device_ids = jnp.arange(N_ROW * N_COL, dtype=jnp.int32)

    def visit_device(running, element):
        device_tiles, row_ids, col_ids, position = element
        global_rows = (position // N_COL * RGB + row_ids).astype(jnp.int32)
        global_cols = (position % N_COL * CGB + col_ids).astype(jnp.int32)
        tiles_wide = device_tiles.astype(jnp.float32)
        if transposed:
            blocks = vector[global_rows].astype(jnp.float32)
            products = jnp.einsum('sab,sa->sb', tiles_wide, blocks)
            return (running.at[global_cols].add(products), None)
        blocks = vector[global_cols].astype(jnp.float32)
        products = jnp.einsum('sab,sb->sa', tiles_wide, blocks)
        return (running.at[global_rows].add(products), None)
    running, _ = lax.scan(visit_device, jnp.zeros((MB, BS), jnp.float32), (flat_tiles, flat_rows, flat_cols, device_ids))
    return running

def reorthogonalize(vectors, image):
    inverse = 1.0 / (MB * BS)
    coefs = jnp.einsum('kmb,mb->k', vectors, image, precision=highest) * inverse
    residual_part = image - jnp.einsum('k,kmb->mb', coefs, vectors, precision=highest)
    meansq = jnp.sum(residual_part * residual_part) * inverse
    norm_val = jnp.sqrt(meansq + eps_floor)
    return (residual_part / norm_val, norm_val)

def reference(matrix_tiles, row_coords, col_coords, left_basis, right_basis):
    left_vectors = left_basis
    right_vectors = right_basis
    alphas = []
    betas = []
    lefts = []
    rights = []
    for iteration in range(ITERS):
        right_now = right_vectors[KB - 1].astype(jnp.bfloat16)
        image = apply_matrix(matrix_tiles, row_coords, col_coords, right_now, False)
        left_new, alpha_val = reorthogonalize(left_vectors, image)
        left_now = left_new.astype(jnp.bfloat16)
        back_image = apply_matrix(matrix_tiles, row_coords, col_coords, left_now, True)
        right_new, beta_val = reorthogonalize(right_vectors, back_image)
        left_vectors = jnp.concatenate([left_vectors[1:], left_new[None]], axis=0)
        right_vectors = jnp.concatenate([right_vectors[1:], right_new[None]], axis=0)
        alphas.append(alpha_val)
        betas.append(beta_val)
        lefts.append(left_new)
        rights.append(right_new)
    bidiagonal = jnp.stack([jnp.stack(alphas), jnp.stack(betas)])
    return (jnp.stack(lefts), jnp.stack(rights), bidiagonal)
```

```python
import functools
import jax
import jax.numpy as jnp
from jax import lax
from jax.experimental import pallas as pl
from jax.experimental.pallas import tpu as pltpu
from jax.sharding import PartitionSpec as P

ITERS = 2
EPS = 1e-6
MESH = pl.DeviceIdType.MESH
NN = (((1,), (0,)), ((), ()))
NT = (((1,), (1,)), ((), ()))
F32 = jnp.float32
BF16 = jnp.bfloat16


def dot(a, b, dims=NN):
    return lax.dot_general(a, b, dims, preferred_element_type=F32)


def floor_div(x, n):
    return jnp.floor((x + 0.5) * (1.0 / n))


def kernel(
    n_rows, n_cols, slots, own, bs, kb,
    tiles, rc, cc, lb, rb,
    nl, nr, bd,
    a_v, idl_s, idl_r, idr_s, idr_r, gl, sl, gr, sr, pm, pmt,
    xs, xr, zs, zr, ps, pr, qs, qr, xp, tc_s, tc_r, tr_s, tr_r,
    a_sem, cs_sem, cr_sem, rs_sem, rr_sem,
):
    i = lax.axis_index("row")
    j = lax.axis_index("col")
    cl = slots // n_cols
    rl = slots // n_rows
    cell = slots // (n_rows * n_cols)
    inverse = 1.0 / (own * bs * n_rows * n_cols)

    def load(b):
        part = pl.ds(b * rl, rl)
        return pltpu.make_async_copy(tiles.at[0, 0, part], a_v.at[part], a_sem.at[b])

    for b in range(n_rows):
        load(b).start()

    barrier = pltpu.get_barrier_semaphore()
    for d in range(1, n_cols):
        pl.semaphore_signal(barrier, inc=1, device_id={"col": lax.rem(j + d, n_cols)}, device_id_type=MESH)
    for d in range(1, n_rows):
        pl.semaphore_signal(barrier, inc=1, device_id={"row": lax.rem(i + d, n_rows)}, device_id_type=MESH)

    sends = []
    axes = {"col": (j, n_cols, cs_sem, cr_sem), "row": (i, n_rows, rs_sem, rr_sem)}
    used = {"col": 0, "row": 0}

    def exchange(axis, src, dst):
        me, n, ssem, rsem = axes[axis]
        phase = used[axis]
        used[axis] += 1
        copies = []
        for d in range(1, n):
            peer = lax.rem(me + d, n)
            copy = pltpu.make_async_remote_copy(
                src_ref=src(peer), dst_ref=dst(me),
                send_sem=ssem.at[phase, d], recv_sem=rsem.at[phase, d],
                device_id={axis: peer}, device_id_type=MESH,
            )
            copy.start()
            sends.append(copy)
            copies.append(copy)

        def wait():
            for copy in copies:
                copy.wait_recv()
        return wait

    def rows_exchange(axis, src, dst):
        me = axes[axis][0]
        n = cl if axis == "col" else rl
        part = lambda ref: lambda p: ref.at[pl.ds(pl.multiple_of(p * n, n), n)]
        wait = exchange(axis, part(src), part(dst))
        mine = pl.ds(pl.multiple_of(me * n, n), n)
        dst[mine, :] = src[mine, :]
        return wait

    def place(s):
        a = floor_div(s, cl)
        q = floor_div(s, cell)
        b = q - n_rows * floor_div(q, n_rows)
        return b * rl + a * cell + (s - q * cell)

    it0 = lax.broadcasted_iota(jnp.int32, (slots, slots), 0).astype(F32)
    it1 = lax.broadcasted_iota(jnp.int32, (slots, slots), 1).astype(F32)
    pm[...] = jnp.where(place(it0) == it1, 1.0, 0.0).astype(BF16)
    pmt[...] = jnp.where(place(it1) == it0, 1.0, 0.0).astype(BF16)

    def column(row):
        return jnp.transpose(jnp.broadcast_to(row, (bs, slots)))

    lane = lax.broadcasted_iota(jnp.int32, (1, slots), 1).astype(F32)
    r_loc = rc[0, 0:1, :].astype(F32) - own * floor_div(lane, cl)
    q = floor_div(lane, cell)
    c_loc = cc[0, 0:1, :].astype(F32) - own * (q - n_rows * floor_div(q, n_rows))
    idl_s[...] = column(r_loc).astype(idl_s.dtype)
    idr_s[...] = dot(pmt[...], column(c_loc).astype(BF16)).astype(BF16)

    pl.semaphore_wait(barrier, n_cols + n_rows - 2)
    wait_r = rows_exchange("row", idr_s, idr_r)
    wait_l = rows_exchange("col", idl_s, idl_r)

    lane8 = lax.broadcasted_iota(jnp.int32, (kb, bs), 1)

    def lanes_to_column(rows):
        return jnp.sum(jnp.concatenate(rows, axis=0), axis=1, keepdims=True)

    def correlate(vectors, target):
        return lanes_to_column([jnp.sum(v[...] * target, axis=0, keepdims=True) for v in vectors])

    left = [lb.at[k] for k in range(kb)]
    right = [rb.at[k] for k in range(kb)]

    all_reduce_count = [0]

    def all_reduce(tile):
        n = all_reduce_count[0]
        all_reduce_count[0] += 1
        tc_s[n] = tile
        tc_r[n, j] = tile
        wait = exchange("col", lambda p: tc_s.at[n], lambda p: tc_r.at[n, p])

        def middle():
            wait()
            total = tc_r[n, 0]
            for k in range(1, n_cols):
                total = total + tc_r[n, k]
            tr_s[n] = total
            tr_r[n, i] = total
            wait2 = exchange("row", lambda p: tr_s.at[n], lambda p: tr_r.at[n, p])

            def final():
                wait2()
                total = tr_r[n, 0]
                for k in range(1, n_rows):
                    total = total + tr_r[n, k]
                return total * inverse
            return final
        return middle

    gram = jnp.zeros((kb, bs), F32)
    for side, vectors in enumerate((right, left)):
        for l in range(kb):
            col = correlate(vectors, vectors[l][...])
            gram = gram + jnp.where(lane8 == side * kb + l, col, 0.0)
        if side == 0:
            def one_hot(idx, g, s):
                halves = [
                    jnp.where(
                        idx[...].astype(F32)
                        == (lax.broadcasted_iota(jnp.int32, (slots, bs), 1) + h * bs).astype(F32),
                        1.0, 0.0)
                    for h in range(own // bs)
                ]
                whole = jnp.concatenate(halves, axis=1)
                g[...] = whole.astype(BF16)
                s[...] = jnp.transpose(whole).astype(BF16)

            wait_r()
            one_hot(idr_r, gr, sr)
            xs[0] = dot(gr[...], rb[kb - 1].astype(BF16)).astype(BF16)
            wait_x = rows_exchange("row", xs.at[0], xr.at[0])
    middle = all_reduce(gram)
    wait_l()
    one_hot(idl_r, gl, sl)
    final = middle()
    grams = None

    row16 = lax.broadcasted_iota(jnp.int32, (16, bs), 0)

    def products(x, out, transposed, first):
        def body(b, carry):
            if first:
                load(b).wait()
            for g in range(rl // 16):
                part = pl.ds(pl.multiple_of(b * rl + g * 16, 16), 16)
                xg = x[part, :].astype(F32)
                acc = jnp.zeros((16, bs), F32)
                for r in range(16):
                    one = jnp.where(row16 == r, xg, 0.0).astype(BF16)
                    k = g * 16 + r
                    if transposed:
                        t = k // cell * cl + b * cell + k % cell
                        acc = acc + dot(one, a_v[t], NN)
                    else:
                        acc = acc + dot(one, a_v[b * rl + k], NT)
                out[part, :] = acc
            return carry
        lax.fori_loop(0, n_rows, body, 0)

    def scatter(s, got):
        value = got[...]
        high = value.astype(BF16)
        rest = value - high.astype(F32)
        mid = rest.astype(BF16)
        low = (rest - mid.astype(F32)).astype(BF16)
        return dot(s[...], high) + dot(s[...], mid) + dot(s[...], low)

    def orthogonal(vectors, image, gram_cols, fresh, out):
        tile = jnp.where(lane8 == 0, correlate(vectors, image), 0.0)
        square = jnp.sum(jnp.sum(image * image, axis=0, keepdims=True), axis=1, keepdims=True)
        tile = tile + jnp.where(lane8 == 1, square, 0.0)
        if fresh is not None:
            tile = tile + fresh
        return tile

    def finish(vectors, image, total, gram_cols, out):
        c = total[:, 0:1]
        p2 = total[0:1, 1:2]
        gc = jnp.zeros((kb, 1), F32)
        part = image
        for k in range(kb):
            ck = c[k:k + 1, :]
            gc = gc + gram_cols[k] * ck
            part = part - ck * vectors[k][...]
        meansq = p2 + jnp.sum(c * gc - 2.0 * c * c, axis=0, keepdims=True)
        norm = jnp.sqrt(jnp.maximum(meansq, 0.0) + EPS)
        new = part * (1.0 / norm)
        out[...] = new
        return new, norm

    def shifted(cols, last):
        sub = lax.broadcasted_iota(jnp.int32, (kb, 1), 0)
        out = []
        for k in range(1, kb):
            moved = jnp.concatenate([cols[k][1:], last[k - 1:k]], axis=0)
            out.append(moved)
        return out + [last]

    norms = []
    for t in range(ITERS):
        wait_x()
        xp[...] = dot(pm[...], xr[t]).astype(BF16)
        products(xp, ps.at[t], False, t == 0)
        wait = rows_exchange("col", ps.at[t], pr.at[t])
        if t == 0:
            g = final()
            gram_r = [g[:, k:k + 1] for k in range(kb)]
            gram_l = [g[:, kb + k:kb + k + 1] for k in range(kb)]
            fresh_l = None
            fresh_r = None
        wait()
        image = scatter(sl, pr.at[t])
        total = all_reduce(orthogonal(left, image, gram_l, fresh_l, None))()()
        if fresh_l is not None:
            gram_l = shifted(gram_l, total[:, 2:3])
        new, alpha = finish(left, image, total, gram_l, nl.at[t])
        left = left[1:] + [nl.at[t]]
        zs[t] = dot(gl[...], new.astype(BF16)).astype(zs.dtype)
        wait = rows_exchange("col", zs.at[t], zr.at[t])
        if t + 1 < ITERS:
            fresh_l = jnp.where(lane8 == 2, correlate(left, new), 0.0)
        wait()
        xp[...] = dot(pmt[...], zr[t].astype(BF16)).astype(BF16)
        products(xp, qs.at[t], True, False)
        wait = rows_exchange("row", qs.at[t], qr.at[t])
        wait()
        image = scatter(sr, qr.at[t])
        total = all_reduce(orthogonal(right, image, gram_r, fresh_r, None))()()
        if fresh_r is not None:
            gram_r = shifted(gram_r, total[:, 2:3])
        new, beta = finish(right, image, total, gram_r, nr.at[t])
        right = right[1:] + [nr.at[t]]
        norms.append((alpha, beta))
        if t + 1 < ITERS:
            xs[t + 1] = dot(gr[...], new.astype(BF16)).astype(BF16)
            wait_x = rows_exchange("row", xs.at[t + 1], xr.at[t + 1])
            fresh_r = jnp.where(lane8 == 2, correlate(right, new), 0.0)

    r2 = lax.broadcasted_iota(jnp.int32, (2, ITERS), 0)
    c2 = lax.broadcasted_iota(jnp.int32, (2, ITERS), 1)
    value = jnp.zeros((2, ITERS), F32)
    for t in range(ITERS):
        for side in range(2):
            value = jnp.where((r2 == side) & (c2 == t), norms[t][side], value)
    bd[...] = value
    for copy in sends:
        copy.wait_send()


def solution(mesh):
    n_rows, n_cols = mesh.shape["row"], mesh.shape["col"]

    def body(tiles, rc, cc, lb, rb):
        _, _, slots, bs, _ = tiles.shape
        kb, own, _ = lb.shape
        wire = BF16 if (slots // n_cols) % 16 == 0 else F32
        reduces = 1 + 2 * ITERS
        vm = lambda shape, dtype: pltpu.VMEM(shape, dtype)
        col_phases = 1 + reduces + 2 * ITERS
        row_phases = 1 + reduces + 2 * ITERS
        ops = [pl.BlockSpec(memory_space=pl.ANY)] + [pl.BlockSpec(memory_space=pltpu.VMEM)] * 4
        return pl.pallas_call(
            functools.partial(kernel, n_rows, n_cols, slots, own, bs, kb),
            out_shape=(
                jax.ShapeDtypeStruct((ITERS, own, bs), F32),
                jax.ShapeDtypeStruct((ITERS, own, bs), F32),
                jax.ShapeDtypeStruct((2, ITERS), F32),
            ),
            in_specs=ops,
            out_specs=(pl.BlockSpec(memory_space=pltpu.VMEM),) * 3,
            scratch_shapes=[
                vm((slots, bs, bs), BF16),
                vm((slots, bs), wire), vm((slots, bs), wire),
                vm((slots, bs), BF16), vm((slots, bs), BF16),
                vm((slots, own), BF16), vm((own, slots), BF16),
                vm((slots, own), BF16), vm((own, slots), BF16),
                vm((slots, slots), BF16), vm((slots, slots), BF16),
                vm((ITERS, slots, bs), BF16), vm((ITERS, slots, bs), BF16),
                vm((ITERS, slots, bs), wire), vm((ITERS, slots, bs), wire),
                vm((ITERS, slots, bs), F32), vm((ITERS, slots, bs), F32),
                vm((ITERS, slots, bs), F32), vm((ITERS, slots, bs), F32),
                vm((slots, bs), BF16),
                vm((reduces, kb, bs), F32), vm((reduces, n_cols, kb, bs), F32),
                vm((reduces, kb, bs), F32), vm((reduces, n_rows, kb, bs), F32),
                pltpu.SemaphoreType.DMA((n_rows,)),
                pltpu.SemaphoreType.DMA((col_phases, n_cols)),
                pltpu.SemaphoreType.DMA((col_phases, n_cols)),
                pltpu.SemaphoreType.DMA((row_phases, n_rows)),
                pltpu.SemaphoreType.DMA((row_phases, n_rows)),
            ],
            compiler_params=pltpu.CompilerParams(
                collective_id=0, has_side_effects=True, vmem_limit_bytes=40 * 1024 * 1024
            ),
            name="lanczos",
        )(tiles, rc, cc, lb, rb)

    in_specs = (
        P("row", "col", None, None, None),
        P("row", "col", None),
        P("row", "col", None),
        P(None, ("row", "col"), None),
        P(None, ("col", "row"), None),
    )
    out_specs = (P(None, ("row", "col"), None), P(None, ("col", "row"), None), P())
    return jax.shard_map(body, mesh=mesh, in_specs=in_specs, out_specs=out_specs, check_vma=False)
```

```python
import functools
import jax
import jax.numpy as jnp
from jax import lax
from jax.experimental import pallas as pl
from jax.experimental.pallas import tpu as pltpu
from jax.sharding import PartitionSpec as P

ITERS = 2
EPS = 1e-6
MESH = pl.DeviceIdType.MESH
NN = (((1,), (0,)), ((), ()))
NT = (((1,), (1,)), ((), ()))
F32 = jnp.float32
BF16 = jnp.bfloat16


def dot(a, b, dims=NN):
    return lax.dot_general(a, b, dims, preferred_element_type=F32)


def floor_div(x, n):
    return jnp.floor((x + 0.5) * (1.0 / n))


def kernel(
    n_rows, n_cols, slots, own, bs, kb,
    tiles, rc_h, cc_h, lb_h, rb_h,
    nl, nr, bd,
    rc, cc, lb, rb, a_v, idl_s, idl_r, idr_s, idr_r, gl, sl, gr, sr, pm, pmt,
    xs, xr, zs, zr, ps, pr, qs, qr, xp, tc_s, tc_r, tr_s, tr_r,
    in_sem, a_sem, cs_sem, cr_sem, rs_sem, rr_sem,
):
    i = lax.axis_index("row")
    j = lax.axis_index("col")
    cl = slots // n_cols
    rl = slots // n_rows
    cell = slots // (n_rows * n_cols)
    inverse = 1.0 / (own * bs * n_rows * n_cols)

    def load(b):
        part = pl.ds(b * rl, rl)
        return pltpu.make_async_copy(tiles.at[0, 0, part], a_v.at[part], a_sem.at[b])

    inputs = [
        pltpu.make_async_copy(src, dst, in_sem.at[k])
        for k, (src, dst) in enumerate(((cc_h, cc), (rc_h, rc), (rb_h, rb), (lb_h, lb)))
    ]
    for copy in inputs:
        copy.start()
    for b in range(n_rows):
        load(b).start()

    barrier = pltpu.get_barrier_semaphore()
    for d in range(1, n_cols):
        pl.semaphore_signal(barrier, inc=1, device_id={"col": lax.rem(j + d, n_cols)}, device_id_type=MESH)
    for d in range(1, n_rows):
        pl.semaphore_signal(barrier, inc=1, device_id={"row": lax.rem(i + d, n_rows)}, device_id_type=MESH)

    sends = []
    axes = {"col": (j, n_cols, cs_sem, cr_sem), "row": (i, n_rows, rs_sem, rr_sem)}
    used = {"col": 0, "row": 0}

    def exchange(axis, src, dst):
        me, n, ssem, rsem = axes[axis]
        phase = used[axis]
        used[axis] += 1
        copies = []
        for d in range(1, n):
            peer = lax.rem(me + d, n)
            copy = pltpu.make_async_remote_copy(
                src_ref=src(peer), dst_ref=dst(me),
                send_sem=ssem.at[phase, d], recv_sem=rsem.at[phase, d],
                device_id={axis: peer}, device_id_type=MESH,
            )
            copy.start()
            sends.append(copy)
            copies.append(copy)

        def wait():
            for copy in copies:
                copy.wait_recv()
        return wait

    def rows_exchange(axis, src, dst):
        me = axes[axis][0]
        n = cl if axis == "col" else rl
        part = lambda ref: lambda p: ref.at[pl.ds(pl.multiple_of(p * n, n), n)]
        wait = exchange(axis, part(src), part(dst))
        mine = pl.ds(pl.multiple_of(me * n, n), n)
        dst[mine, :] = src[mine, :]
        return wait

    def place(s):
        a = floor_div(s, cl)
        q = floor_div(s, cell)
        b = q - n_rows * floor_div(q, n_rows)
        return b * rl + a * cell + (s - q * cell)

    it0 = lax.broadcasted_iota(jnp.int32, (slots, slots), 0).astype(F32)
    it1 = lax.broadcasted_iota(jnp.int32, (slots, slots), 1).astype(F32)
    down = place(lax.broadcasted_iota(jnp.int32, (slots, 1), 0).astype(F32))
    across = place(lax.broadcasted_iota(jnp.int32, (1, slots), 1).astype(F32))
    pmt[...] = jnp.where(across == it0, 1.0, 0.0).astype(BF16)
    inputs[0].wait()
    inputs[1].wait()

    def column(row):
        return jnp.transpose(jnp.broadcast_to(row, (bs, slots)))

    lane = lax.broadcasted_iota(jnp.int32, (1, slots), 1).astype(F32)
    r_loc = rc[0, 0:1, :].astype(F32) - own * floor_div(lane, cl)
    q = floor_div(lane, cell)
    c_loc = cc[0, 0:1, :].astype(F32) - own * (q - n_rows * floor_div(q, n_rows))
    idl_s[...] = column(r_loc).astype(idl_s.dtype)
    idr_s[...] = dot(pmt[...], column(c_loc).astype(BF16)).astype(BF16)

    pl.semaphore_wait(barrier, n_cols + n_rows - 2)
    wait_r = rows_exchange("row", idr_s, idr_r)
    wait_l = rows_exchange("col", idl_s, idl_r)

    pm[...] = jnp.where(down == it1, 1.0, 0.0).astype(BF16)
    inputs[2].wait()

    lane8 = lax.broadcasted_iota(jnp.int32, (kb, bs), 1)

    def lanes_to_column(rows):
        return jnp.sum(jnp.concatenate(rows, axis=0), axis=1, keepdims=True)

    def correlate(vectors, target):
        return lanes_to_column([jnp.sum(v[...] * target, axis=0, keepdims=True) for v in vectors])

    left = [lb.at[k] for k in range(kb)]
    right = [rb.at[k] for k in range(kb)]

    all_reduce_count = [0]

    def all_reduce(tile):
        n = all_reduce_count[0]
        all_reduce_count[0] += 1
        tc_s[n] = tile
        tc_r[n, j] = tile
        wait = exchange("col", lambda p: tc_s.at[n], lambda p: tc_r.at[n, p])

        def middle():
            wait()
            total = tc_r[n, 0]
            for k in range(1, n_cols):
                total = total + tc_r[n, k]
            tr_s[n] = total
            tr_r[n, i] = total
            wait2 = exchange("row", lambda p: tr_s.at[n], lambda p: tr_r.at[n, p])

            def final():
                wait2()
                total = tr_r[n, 0]
                for k in range(1, n_rows):
                    total = total + tr_r[n, k]
                return total * inverse
            return final
        return middle

    gram = jnp.zeros((kb, bs), F32)
    for side, vectors in enumerate((right, left)):
        if side == 1:
            inputs[3].wait()
        for l in range(kb):
            col = correlate(vectors, vectors[l][...])
            gram = gram + jnp.where(lane8 == side * kb + l, col, 0.0)
        if side == 0:
            def one_hot(idx, g, s):
                halves = [
                    jnp.where(
                        idx[...].astype(F32)
                        == (lax.broadcasted_iota(jnp.int32, (slots, bs), 1) + h * bs).astype(F32),
                        1.0, 0.0)
                    for h in range(own // bs)
                ]
                whole = jnp.concatenate(halves, axis=1)
                g[...] = whole.astype(BF16)
                s[...] = jnp.transpose(whole).astype(BF16)

            wait_r()
            one_hot(idr_r, gr, sr)
            xs[0] = dot(gr[...], rb[kb - 1].astype(BF16)).astype(BF16)
            wait_x = rows_exchange("row", xs.at[0], xr.at[0])
    middle = all_reduce(gram)
    wait_l()
    one_hot(idl_r, gl, sl)
    final = middle()
    grams = None

    for b in range(n_rows):
        load(b).wait()

    def products(x, out, dst, axis):
        me, n, ssem, rsem = axes[axis]
        phase = used[axis]
        used[axis] += 1
        chunk = cl if axis == "col" else rl
        group = 16 if chunk % 16 == 0 else 8
        row_id = lax.broadcasted_iota(jnp.int32, (group, bs), 0)
        mine = pl.ds(pl.multiple_of(me * chunk, chunk), chunk)

        def copy(d):
            peer = lax.rem(me + d, n)
            return pltpu.make_async_remote_copy(
                src_ref=out.at[pl.ds(pl.multiple_of(peer * chunk, chunk), chunk)], dst_ref=dst.at[mine],
                send_sem=ssem.at[phase, d], recv_sem=rsem.at[phase, d],
                device_id={axis: peer}, device_id_type=MESH,
            )

        def body(d, carry):
            p = lax.rem(me + d, n)
            for g in range(chunk // group):
                part = pl.ds(pl.multiple_of(p * chunk + g * group, group), group)
                xg = x[part, :]
                lhs = jnp.concatenate(
                    [jnp.where(row_id == r, xg, 0.0).astype(BF16) for r in range(group)], axis=1)
                if axis == "col":
                    rhs = a_v[pl.ds(p * chunk + g * group, group)].reshape(group * bs, bs)
                else:
                    ks = range(g * group, (g + 1) * group)
                    rhs = jnp.concatenate([a_v[k // cell * cl + p * cell + k % cell] for k in ks], axis=0)
                if axis == "col":
                    o = dot(xg.astype(BF16), rhs, NT)
                    acc = jnp.zeros((group, bs), F32)
                    for r in range(group):
                        acc = acc + jnp.where(row_id == r, o[:, r * bs:(r + 1) * bs], 0.0)
                    out[part, :] = acc
                else:
                    out[part, :] = dot(lhs, rhs)

            @pl.when(d < n)
            def _():
                copy(d).start()
            return carry
        lax.fori_loop(1, n + 1, body, 0)
        dst[mine, :] = out[mine, :]
        copies = [copy(d) for d in range(1, n)]
        sends.extend(copies)

        def wait():
            for c in copies:
                c.wait_recv()
        return wait

    def scatter(s, got):
        value = got[...]
        high = value.astype(BF16)
        rest = value - high.astype(F32)
        mid = rest.astype(BF16)
        low = (rest - mid.astype(F32)).astype(BF16)
        return dot(s[...], high) + dot(s[...], mid) + dot(s[...], low)

    def sums(vectors, image, fresh):
        tile = jnp.where(lane8 == 0, correlate(vectors, image), 0.0)
        square = jnp.sum(jnp.sum(image * image, axis=0, keepdims=True), axis=1, keepdims=True)
        tile = tile + jnp.where(lane8 == 1, square, 0.0)
        return tile if fresh is None else tile + fresh

    def finish(vectors, image, total, gram_cols, out):
        c = total[:, 0:1]
        p2 = total[0:1, 1:2]
        gc = jnp.zeros((kb, 1), F32)
        part = image
        for k in range(kb):
            ck = c[k:k + 1, :]
            gc = gc + gram_cols[k] * ck
            part = part - ck * vectors[k][...]
        meansq = p2 + jnp.sum(c * gc - 2.0 * c * c, axis=0, keepdims=True)
        norm = jnp.sqrt(jnp.maximum(meansq, 0.0) + EPS)
        new = part * (1.0 / norm)
        out[...] = new
        return new, norm

    def shifted(cols, last):
        sub = lax.broadcasted_iota(jnp.int32, (kb, 1), 0)
        out = []
        for k in range(1, kb):
            moved = jnp.concatenate([cols[k][1:], last[k - 1:k]], axis=0)
            out.append(moved)
        return out + [last]

    norms = []
    for t in range(ITERS):
        wait_x()
        xp[...] = dot(pm[...], xr[t])
        wait = products(xp, ps.at[t], pr.at[t], "col")
        if t == 0:
            g = final()
            gram_r = [g[:, k:k + 1] for k in range(kb)]
            gram_l = [g[:, kb + k:kb + k + 1] for k in range(kb)]
            fresh_l = None
            fresh_r = None
        wait()
        image = scatter(sl, pr.at[t])
        total = all_reduce(sums(left, image, fresh_l))()()
        if fresh_l is not None:
            gram_l = shifted(gram_l, total[:, 2:3])
        new, alpha = finish(left, image, total, gram_l, nl.at[t])
        left = left[1:] + [nl.at[t]]
        zs[t] = dot(gl[...], new.astype(BF16)).astype(zs.dtype)
        wait = rows_exchange("col", zs.at[t], zr.at[t])
        if t + 1 < ITERS:
            fresh_l = jnp.where(lane8 == 2, correlate(left, new), 0.0)
        wait()
        xp[...] = dot(pmt[...], zr[t].astype(BF16))
        wait = products(xp, qs.at[t], qr.at[t], "row")
        wait()
        image = scatter(sr, qr.at[t])
        total = all_reduce(sums(right, image, fresh_r))()()
        if fresh_r is not None:
            gram_r = shifted(gram_r, total[:, 2:3])
        new, beta = finish(right, image, total, gram_r, nr.at[t])
        right = right[1:] + [nr.at[t]]
        norms.append((alpha, beta))
        if t + 1 < ITERS:
            xs[t + 1] = dot(gr[...], new.astype(BF16)).astype(BF16)
            wait_x = rows_exchange("row", xs.at[t + 1], xr.at[t + 1])
            fresh_r = jnp.where(lane8 == 2, correlate(right, new), 0.0)

    r2 = lax.broadcasted_iota(jnp.int32, (2, ITERS), 0)
    c2 = lax.broadcasted_iota(jnp.int32, (2, ITERS), 1)
    value = jnp.zeros((2, ITERS), F32)
    for t in range(ITERS):
        for side in range(2):
            value = jnp.where((r2 == side) & (c2 == t), norms[t][side], value)
    bd[...] = value
    for copy in sends:
        copy.wait_send()


def solution(mesh):
    n_rows, n_cols = mesh.shape["row"], mesh.shape["col"]

    def body(tiles, rc, cc, lb, rb):
        _, _, slots, bs, _ = tiles.shape
        kb, own, _ = lb.shape
        wire = BF16 if (slots // n_cols) % 16 == 0 else F32
        reduces = 1 + 2 * ITERS
        vm = lambda shape, dtype: pltpu.VMEM(shape, dtype)
        col_phases = 1 + reduces + 2 * ITERS
        row_phases = 1 + reduces + 2 * ITERS
        ops = [pl.BlockSpec(memory_space=pl.ANY)] * 5
        return pl.pallas_call(
            functools.partial(kernel, n_rows, n_cols, slots, own, bs, kb),
            out_shape=(
                jax.ShapeDtypeStruct((ITERS, own, bs), F32),
                jax.ShapeDtypeStruct((ITERS, own, bs), F32),
                jax.ShapeDtypeStruct((2, ITERS), F32),
            ),
            in_specs=ops,
            out_specs=(pl.BlockSpec(memory_space=pltpu.VMEM),) * 3,
            scratch_shapes=[
                vm(rc.shape, jnp.int32), vm(cc.shape, jnp.int32), vm(lb.shape, F32), vm(rb.shape, F32),
                vm((slots, bs, bs), BF16),
                vm((slots, bs), wire), vm((slots, bs), wire),
                vm((slots, bs), BF16), vm((slots, bs), BF16),
                vm((slots, own), BF16), vm((own, slots), BF16),
                vm((slots, own), BF16), vm((own, slots), BF16),
                vm((slots, slots), BF16), vm((slots, slots), BF16),
                vm((ITERS, slots, bs), BF16), vm((ITERS, slots, bs), BF16),
                vm((ITERS, slots, bs), wire), vm((ITERS, slots, bs), wire),
                vm((ITERS, slots, bs), F32), vm((ITERS, slots, bs), F32),
                vm((ITERS, slots, bs), F32), vm((ITERS, slots, bs), F32),
                vm((slots, bs), F32),
                vm((reduces, kb, bs), F32), vm((reduces, n_cols, kb, bs), F32),
                vm((reduces, kb, bs), F32), vm((reduces, n_rows, kb, bs), F32),
                pltpu.SemaphoreType.DMA((4,)),
                pltpu.SemaphoreType.DMA((n_rows,)),
                pltpu.SemaphoreType.DMA((col_phases, n_cols)),
                pltpu.SemaphoreType.DMA((col_phases, n_cols)),
                pltpu.SemaphoreType.DMA((row_phases, n_rows)),
                pltpu.SemaphoreType.DMA((row_phases, n_rows)),
            ],
            compiler_params=pltpu.CompilerParams(
                collective_id=0, has_side_effects=True, vmem_limit_bytes=52 * 1024 * 1024
            ),
            name="lanczos",
        )(tiles, rc, cc, lb, rb)

    in_specs = (
        P("row", "col", None, None, None),
        P("row", "col", None),
        P("row", "col", None),
        P(None, ("row", "col"), None),
        P(None, ("col", "row"), None),
    )
    out_specs = (P(None, ("row", "col"), None), P(None, ("col", "row"), None), P())
    return jax.shard_map(body, mesh=mesh, in_specs=in_specs, out_specs=out_specs, check_vma=False)
```

```python
import functools
import jax
import jax.numpy as jnp
from jax import lax
from jax.experimental import pallas as pl
from jax.experimental.pallas import tpu as pltpu
from jax.sharding import PartitionSpec as P

ITERS = 2
EPS = 1e-6
MESH = pl.DeviceIdType.MESH
NN = (((1,), (0,)), ((), ()))
NT = (((1,), (1,)), ((), ()))
F32 = jnp.float32
BF16 = jnp.bfloat16


def dot(a, b, dims=NN):
    return lax.dot_general(a, b, dims, preferred_element_type=F32)


def floor_div(x, n):
    return jnp.floor((x + 0.5) * (1.0 / n))


def kernel(
    n_rows, n_cols, slots, own, bs, kb,
    tiles, rc_h, cc_h, lb_h, rb_h,
    nl, nr, bd,
    rc, cc, lb, rb, a_v, idl_s, idl_r, idr_s, idr_r, gl, sl, gr, sr, pm, pmt,
    xs, xr, zs, zr, ps, pr, qs, qr, xp, tc_s, tc_r, tr_s, tr_r,
    in_sem, a_sem, cs_sem, cr_sem, rs_sem, rr_sem, as_sem, ar_sem,
):
    i = lax.axis_index("row")
    j = lax.axis_index("col")
    cl = slots // n_cols
    rl = slots // n_rows
    cell = slots // (n_rows * n_cols)
    inverse = 1.0 / (own * bs * n_rows * n_cols)

    def load(b):
        part = pl.ds(b * rl, rl)
        return pltpu.make_async_copy(tiles.at[0, 0, part], a_v.at[part], a_sem.at[b])

    inputs = [
        pltpu.make_async_copy(src, dst, in_sem.at[k])
        for k, (src, dst) in enumerate(((cc_h, cc), (rc_h, rc), (rb_h, rb), (lb_h, lb)))
    ]
    for copy in inputs:
        copy.start()
    for b in range(n_rows):
        load(b).start()

    barrier = pltpu.get_barrier_semaphore()
    n_all = n_rows * n_cols
    me_all = i * n_cols + j
    one_stage = n_all <= 32

    def device(axis, me, d):
        if axis == "all":
            peer = lax.rem(me + d, n_all)
            return {"row": peer // n_cols, "col": lax.rem(peer, n_cols)}
        return {axis: lax.rem(me + d, n_cols if axis == "col" else n_rows)}

    greeted = (("all", me_all, n_all),) if one_stage else (("col", j, n_cols), ("row", i, n_rows))
    for axis, me, n in greeted:
        for d in range(1, n):
            pl.semaphore_signal(barrier, inc=1, device_id=device(axis, me, d), device_id_type=MESH)

    sends = []
    axes = {
        "col": (j, n_cols, cs_sem, cr_sem),
        "row": (i, n_rows, rs_sem, rr_sem),
        "all": (me_all, n_all, as_sem, ar_sem),
    }
    used = {"col": 0, "row": 0, "all": 0}

    def exchange(axis, src, dst):
        me, n, ssem, rsem = axes[axis]
        phase = used[axis]
        used[axis] += 1
        copies = []
        for d in range(1, n):
            peer = lax.rem(me + d, n)
            copy = pltpu.make_async_remote_copy(
                src_ref=src(peer), dst_ref=dst(me),
                send_sem=ssem.at[phase, d], recv_sem=rsem.at[phase, d],
                device_id=device(axis, me, d), device_id_type=MESH,
            )
            copy.start()
            sends.append(copy)
            copies.append(copy)

        def wait():
            for copy in copies:
                copy.wait_recv()
        return wait

    def rows_exchange(axis, src, dst):
        me = axes[axis][0]
        n = cl if axis == "col" else rl
        part = lambda ref: lambda p: ref.at[pl.ds(pl.multiple_of(p * n, n), n)]
        wait = exchange(axis, part(src), part(dst))
        mine = pl.ds(pl.multiple_of(me * n, n), n)
        dst[mine, :] = src[mine, :]
        return wait

    def place(s):
        a = floor_div(s, cl)
        q = floor_div(s, cell)
        b = q - n_rows * floor_div(q, n_rows)
        return b * rl + a * cell + (s - q * cell)

    it0 = lax.broadcasted_iota(jnp.int32, (slots, slots), 0).astype(F32)
    it1 = lax.broadcasted_iota(jnp.int32, (slots, slots), 1).astype(F32)
    down = place(lax.broadcasted_iota(jnp.int32, (slots, 1), 0).astype(F32))
    across = place(lax.broadcasted_iota(jnp.int32, (1, slots), 1).astype(F32))
    pmt[...] = jnp.where(across == it0, 1.0, 0.0).astype(BF16)
    inputs[0].wait()
    inputs[1].wait()

    def column(row):
        return jnp.transpose(jnp.broadcast_to(row, (bs, slots)))

    lane = lax.broadcasted_iota(jnp.int32, (1, slots), 1).astype(F32)
    r_loc = rc[0, 0:1, :].astype(F32) - own * floor_div(lane, cl)
    q = floor_div(lane, cell)
    c_loc = cc[0, 0:1, :].astype(F32) - own * (q - n_rows * floor_div(q, n_rows))
    idl_s[...] = column(r_loc).astype(idl_s.dtype)
    idr_s[...] = dot(pmt[...], column(c_loc).astype(BF16)).astype(BF16)

    pl.semaphore_wait(barrier, n_all - 1 if one_stage else n_cols + n_rows - 2)
    wait_r = rows_exchange("row", idr_s, idr_r)
    wait_l = rows_exchange("col", idl_s, idl_r)

    pm[...] = jnp.where(down == it1, 1.0, 0.0).astype(BF16)
    inputs[2].wait()

    lane8 = lax.broadcasted_iota(jnp.int32, (kb, bs), 1)

    def lanes_to_column(rows):
        return jnp.sum(jnp.concatenate(rows, axis=0), axis=1, keepdims=True)

    def correlate(vectors, target):
        return lanes_to_column([jnp.sum(v[...] * target, axis=0, keepdims=True) for v in vectors])

    left = [lb.at[k] for k in range(kb)]
    right = [rb.at[k] for k in range(kb)]

    all_reduce_count = [0]

    def all_reduce(tile):
        n = all_reduce_count[0]
        all_reduce_count[0] += 1
        tc_s[n] = tile
        if one_stage:
            tr_r[n, me_all] = tile
            wait_all = exchange("all", lambda p: tc_s.at[n], lambda p: tr_r.at[n, p])

            def last():
                wait_all()
                return jnp.sum(tr_r[n], axis=0) * inverse
            return lambda: last
        tc_r[n, j] = tile
        wait = exchange("col", lambda p: tc_s.at[n], lambda p: tc_r.at[n, p])

        def middle():
            wait()
            total = tc_r[n, 0]
            for k in range(1, n_cols):
                total = total + tc_r[n, k]
            tr_s[n] = total
            tr_r[n, i] = total
            wait2 = exchange("row", lambda p: tr_s.at[n], lambda p: tr_r.at[n, p])

            def final():
                wait2()
                total = tr_r[n, 0]
                for k in range(1, n_rows):
                    total = total + tr_r[n, k]
                return total * inverse
            return final
        return middle

    gram = jnp.zeros((kb, bs), F32)
    for side, vectors in enumerate((right, left)):
        if side == 1:
            inputs[3].wait()
        for l in range(kb):
            col = correlate(vectors, vectors[l][...])
            gram = gram + jnp.where(lane8 == side * kb + l, col, 0.0)
        if side == 0:
            def one_hot(idx, g, s):
                halves = [
                    jnp.where(
                        idx[...].astype(F32)
                        == (lax.broadcasted_iota(jnp.int32, (slots, bs), 1) + h * bs).astype(F32),
                        1.0, 0.0)
                    for h in range(own // bs)
                ]
                whole = jnp.concatenate(halves, axis=1)
                g[...] = whole.astype(BF16)
                s[...] = jnp.transpose(whole).astype(BF16)

            wait_r()
            one_hot(idr_r, gr, sr)
            xs[0] = dot(gr[...], rb[kb - 1].astype(BF16)).astype(BF16)
            wait_x = rows_exchange("row", xs.at[0], xr.at[0])
    middle = all_reduce(gram)
    wait_l()
    one_hot(idl_r, gl, sl)
    final = middle()
    grams = None

    for b in range(n_rows):
        load(b).wait()

    def products(x, out, dst, axis):
        me, n, ssem, rsem = axes[axis]
        phase = used[axis]
        used[axis] += 1
        chunk = cl if axis == "col" else rl
        group = 16 if chunk % 16 == 0 else 8
        row_id = lax.broadcasted_iota(jnp.int32, (group, bs), 0)
        mine = pl.ds(pl.multiple_of(me * chunk, chunk), chunk)

        def copy(d):
            peer = lax.rem(me + d, n)
            return pltpu.make_async_remote_copy(
                src_ref=out.at[pl.ds(pl.multiple_of(peer * chunk, chunk), chunk)], dst_ref=dst.at[mine],
                send_sem=ssem.at[phase, d], recv_sem=rsem.at[phase, d],
                device_id={axis: peer}, device_id_type=MESH,
            )

        def body(d, carry):
            p = lax.rem(me + d, n)
            for g in range(chunk // group):
                part = pl.ds(pl.multiple_of(p * chunk + g * group, group), group)
                xg = x[part, :]
                lhs = jnp.concatenate(
                    [jnp.where(row_id == r, xg, 0.0).astype(BF16) for r in range(group)], axis=1)
                if axis == "col":
                    rhs = a_v[pl.ds(p * chunk + g * group, group)].reshape(group * bs, bs)
                else:
                    ks = range(g * group, (g + 1) * group)
                    rhs = jnp.concatenate([a_v[k // cell * cl + p * cell + k % cell] for k in ks], axis=0)
                if axis == "col":
                    o = dot(xg.astype(BF16), rhs, NT)
                    acc = jnp.zeros((group, bs), F32)
                    for r in range(group):
                        acc = acc + jnp.where(row_id == r, o[:, r * bs:(r + 1) * bs], 0.0)
                    out[part, :] = acc
                else:
                    out[part, :] = dot(lhs, rhs)

            @pl.when(d < n)
            def _():
                copy(d).start()
            return carry
        lax.fori_loop(1, n + 1, body, 0)
        dst[mine, :] = out[mine, :]
        copies = [copy(d) for d in range(1, n)]
        sends.extend(copies)

        def wait():
            for c in copies:
                c.wait_recv()
        return wait

    def scatter(s, got):
        value = got[...]
        high = value.astype(BF16)
        rest = value - high.astype(F32)
        mid = rest.astype(BF16)
        low = (rest - mid.astype(F32)).astype(BF16)
        return dot(s[...], high) + dot(s[...], mid) + dot(s[...], low)

    def sums(vectors, image, fresh):
        tile = jnp.where(lane8 == 0, correlate(vectors, image), 0.0)
        square = jnp.sum(jnp.sum(image * image, axis=0, keepdims=True), axis=1, keepdims=True)
        tile = tile + jnp.where(lane8 == 1, square, 0.0)
        return tile if fresh is None else tile + fresh

    def finish(vectors, image, total, gram_cols, out):
        c = total[:, 0:1]
        p2 = total[0:1, 1:2]
        gc = jnp.zeros((kb, 1), F32)
        part = image
        for k in range(kb):
            ck = c[k:k + 1, :]
            gc = gc + gram_cols[k] * ck
            part = part - ck * vectors[k][...]
        meansq = p2 + jnp.sum(c * gc - 2.0 * c * c, axis=0, keepdims=True)
        norm = jnp.sqrt(jnp.maximum(meansq, 0.0) + EPS)
        new = part * (1.0 / norm)
        out[...] = new
        return new, norm

    def shifted(cols, last):
        sub = lax.broadcasted_iota(jnp.int32, (kb, 1), 0)
        out = []
        for k in range(1, kb):
            moved = jnp.concatenate([cols[k][1:], last[k - 1:k]], axis=0)
            out.append(moved)
        return out + [last]

    norms = []
    for t in range(ITERS):
        wait_x()
        xp[...] = dot(pm[...], xr[t])
        wait = products(xp, ps.at[t], pr.at[t], "col")
        if t == 0:
            g = final()
            gram_r = [g[:, k:k + 1] for k in range(kb)]
            gram_l = [g[:, kb + k:kb + k + 1] for k in range(kb)]
            fresh_l = None
            fresh_r = None
        wait()
        image = scatter(sl, pr.at[t])
        total = all_reduce(sums(left, image, fresh_l))()()
        if fresh_l is not None:
            gram_l = shifted(gram_l, total[:, 2:3])
        new, alpha = finish(left, image, total, gram_l, nl.at[t])
        left = left[1:] + [nl.at[t]]
        zs[t] = dot(gl[...], new.astype(BF16)).astype(zs.dtype)
        wait = rows_exchange("col", zs.at[t], zr.at[t])
        if t + 1 < ITERS:
            fresh_l = jnp.where(lane8 == 2, correlate(left, new), 0.0)
        wait()
        xp[...] = dot(pmt[...], zr[t].astype(BF16))
        wait = products(xp, qs.at[t], qr.at[t], "row")
        wait()
        image = scatter(sr, qr.at[t])
        total = all_reduce(sums(right, image, fresh_r))()()
        if fresh_r is not None:
            gram_r = shifted(gram_r, total[:, 2:3])
        new, beta = finish(right, image, total, gram_r, nr.at[t])
        right = right[1:] + [nr.at[t]]
        norms.append((alpha, beta))
        if t + 1 < ITERS:
            xs[t + 1] = dot(gr[...], new.astype(BF16)).astype(BF16)
            wait_x = rows_exchange("row", xs.at[t + 1], xr.at[t + 1])
            fresh_r = jnp.where(lane8 == 2, correlate(right, new), 0.0)

    r2 = lax.broadcasted_iota(jnp.int32, (2, ITERS), 0)
    c2 = lax.broadcasted_iota(jnp.int32, (2, ITERS), 1)
    value = jnp.zeros((2, ITERS), F32)
    for t in range(ITERS):
        for side in range(2):
            value = jnp.where((r2 == side) & (c2 == t), norms[t][side], value)
    bd[...] = value
    for copy in sends:
        copy.wait_send()


def solution(mesh):
    n_rows, n_cols = mesh.shape["row"], mesh.shape["col"]

    def body(tiles, rc, cc, lb, rb):
        _, _, slots, bs, _ = tiles.shape
        kb, own, _ = lb.shape
        wire = BF16 if (slots // n_cols) % 16 == 0 else F32
        reduces = 1 + 2 * ITERS
        n_all = n_rows * n_cols
        one_stage = n_all <= 32
        vm = lambda shape, dtype: pltpu.VMEM(shape, dtype)
        col_phases = 1 + reduces + 2 * ITERS
        row_phases = 1 + reduces + 2 * ITERS
        ops = [pl.BlockSpec(memory_space=pl.ANY)] * 5
        return pl.pallas_call(
            functools.partial(kernel, n_rows, n_cols, slots, own, bs, kb),
            out_shape=(
                jax.ShapeDtypeStruct((ITERS, own, bs), F32),
                jax.ShapeDtypeStruct((ITERS, own, bs), F32),
                jax.ShapeDtypeStruct((2, ITERS), F32),
            ),
            in_specs=ops,
            out_specs=(pl.BlockSpec(memory_space=pltpu.VMEM),) * 3,
            scratch_shapes=[
                vm(rc.shape, jnp.int32), vm(cc.shape, jnp.int32), vm(lb.shape, F32), vm(rb.shape, F32),
                vm((slots, bs, bs), BF16),
                vm((slots, bs), wire), vm((slots, bs), wire),
                vm((slots, bs), BF16), vm((slots, bs), BF16),
                vm((slots, own), BF16), vm((own, slots), BF16),
                vm((slots, own), BF16), vm((own, slots), BF16),
                vm((slots, slots), BF16), vm((slots, slots), BF16),
                vm((ITERS, slots, bs), BF16), vm((ITERS, slots, bs), BF16),
                vm((ITERS, slots, bs), wire), vm((ITERS, slots, bs), wire),
                vm((ITERS, slots, bs), F32), vm((ITERS, slots, bs), F32),
                vm((ITERS, slots, bs), F32), vm((ITERS, slots, bs), F32),
                vm((slots, bs), F32),
                vm((reduces, kb, bs), F32), vm((reduces, n_cols, kb, bs), F32),
                vm((reduces, kb, bs), F32), vm((reduces, n_all if one_stage else n_rows, kb, bs), F32),
                pltpu.SemaphoreType.DMA((4,)),
                pltpu.SemaphoreType.DMA((n_rows,)),
                pltpu.SemaphoreType.DMA((col_phases, n_cols)),
                pltpu.SemaphoreType.DMA((col_phases, n_cols)),
                pltpu.SemaphoreType.DMA((row_phases, n_rows)),
                pltpu.SemaphoreType.DMA((row_phases, n_rows)),
                pltpu.SemaphoreType.DMA((reduces, n_all) if one_stage else (1, 1)),
                pltpu.SemaphoreType.DMA((reduces, n_all) if one_stage else (1, 1)),
            ],
            compiler_params=pltpu.CompilerParams(
                collective_id=0, has_side_effects=True, vmem_limit_bytes=52 * 1024 * 1024
            ),
            name="lanczos",
        )(tiles, rc, cc, lb, rb)

    in_specs = (
        P("row", "col", None, None, None),
        P("row", "col", None),
        P("row", "col", None),
        P(None, ("row", "col"), None),
        P(None, ("col", "row"), None),
    )
    out_specs = (P(None, ("row", "col"), None), P(None, ("col", "row"), None), P())
    return jax.shard_map(body, mesh=mesh, in_specs=in_specs, out_specs=out_specs, check_vma=False)
```
